128 devices in a mesh: gx: 4 (over x_hi, core), dev: 32 (over z, y, x_lo).
Axes of the slice: x: 4 (x_hi: 2, x_lo: 2; x = x_hi * 2 + x_lo), y: 4, z: 4, core: 2. Of those that a mesh axis runs over, the one named last changes fastest.
Arguments:
- volume: float32 [64, 128, 4096], P('gx', 'dev'), may hold values from -60 to 60
- occupancy: int32 [8, 32], P('gx', 'dev'), may hold values 0 or 1
Outputs:
- structure: float32 [6, 64, 128, 4096], P(None, 'gx', 'dev')
The draws below stay inside these ranges and needn't reach their ends.
All inputs are finite; a program needn't handle non-finite values. No bound on the sum of `occupancy` on one device may be relied on, other than what follows from the above.
Results may differ from the reference program's by a relative error of at most 0.00002.
Values sent between devices are 32-bit elements; how exact they have to be, the bound alone decides.
No kernel may reach another device: no remote copies, remote signals or barrier semaphores. Data moves between devices by JAX's collectives and lax.ppermute only.
A program may use at most 256 MiB of HBM per device.

```python
import math
import jax
import jax.numpy as jnp
from jax import lax

RAD_D = 3
RAD_S = 12
BRICK_X = 8
BRICK_Z = 4
NX = 64
NZ = 128
NY = 4096


def place_ends(array, rng, low, top_value):
    spot = [jax.random.randint(jax.random.fold_in(rng, axis), (), 0, length) for axis, length in enumerate(array.shape)]
    main_axis = array.shape.index(max(array.shape))
    next_to = spot[:main_axis] + [(spot[main_axis] + 1) % array.shape[main_axis]] + spot[main_axis + 1:]
    return array.at[tuple(spot)].set(low).at[tuple(next_to)].set(top_value)


def steps_of(key, shape, pieces, smallest, top_value):
    level = 1.0
    for dim, shards_of in pieces:
        draws = jax.random.uniform(jax.random.fold_in(jax.random.fold_in(key, 6), dim), (shards_of,), jnp.float32, smallest / len(pieces), top_value / len(pieces))
        level = level * jnp.repeat(jnp.exp(draws), shape[dim] // shards_of).reshape((-1,) + (1,) * (len(shape) - 1 - dim))
    return level


def scatter_about(key, shape, spread, bound, pieces=(), kind=jnp.bfloat16):
    drawn = jax.random.normal(key, shape, jnp.float32) * spread
    if len(pieces) > 0:
        drawn = steps_of(key, shape, pieces, -0.22, 0.18) * drawn
    return jnp.clip(drawn, min=-bound, max=bound).astype(kind)


def setup_inputs(seed: int = 0) -> dict:
    keys = jax.random.split(jax.random.key(seed), 3)
    volume = scatter_about(keys[0], (NX, NZ, NY), 10.0, 60.0, ((0, 4), (1, 32)), jnp.float32)
    occupancy = place_ends((jax.random.randint(keys[1], (NX // BRICK_X, NZ // BRICK_Z), 0, 4) < 3).astype(jnp.int32), jax.random.fold_in(keys[1], 1), 0, 1)
    return dict(volume=volume, occupancy=occupancy)


SIGMA_DERIV = 1.0
SIGMA_SMOOTH = 4.0


def kernel_taps(radius, width_sigma, derivative):
    offsets = [float(t) for t in range(-radius, radius + 1)]
    weights = [math.exp(-0.5 * (t / width_sigma) ** 2) for t in offsets]
    if derivative:
        total = sum(t * t * w for t, w in zip(offsets, weights))
        return [t * w / total for t, w in zip(offsets, weights)]
    total = sum(weights)
    return [w / total for w in weights]


def line_pass(source, weights, dimension):
    length_out = source.shape[dimension] - len(weights) + 1
    summed = float(weights[0]) * lax.slice_in_dim(source, 0, length_out, axis=dimension)
    for offset in range(1, len(weights)):
        summed = summed + float(weights[offset]) * lax.slice_in_dim(source, offset, offset + length_out, axis=dimension)
    return summed


def line_filter(source, weights, dimension):
    radius = (len(weights) - 1) // 2
    widths = [(0, 0)] * source.ndim
    widths[dimension] = (radius, radius)
    return line_pass(jnp.pad(source, widths), weights, dimension)


def reference(volume, occupancy):
    smooth_d = kernel_taps(RAD_D, SIGMA_DERIV, False)
    deriv_d = kernel_taps(RAD_D, SIGMA_DERIV, True)
    smooth_s = kernel_taps(RAD_S, SIGMA_SMOOTH, False)
    presence = jnp.repeat(jnp.repeat(occupancy, BRICK_X, 0), BRICK_Z, 1).astype(jnp.float32)
    masked = volume * presence[:, :, None]
    depth_smooth = line_filter(masked, smooth_d, 1)
    depth_deriv = line_filter(masked, deriv_d, 1)
    grad_x = line_filter(line_filter(depth_smooth, smooth_d, 2), deriv_d, 0)
    grad_y = line_filter(line_filter(depth_smooth, deriv_d, 2), smooth_d, 0)
    grad_z = line_filter(line_filter(depth_deriv, smooth_d, 2), smooth_d, 0)
    products = [grad_x * grad_x, grad_x * grad_y, grad_x * grad_z, grad_y * grad_y, grad_y * grad_z, grad_z * grad_z]
    results = []
    for product in products:
        results.append(line_filter(line_filter(line_filter(product, smooth_s, 2), smooth_s, 0), smooth_s, 1))
    return jnp.stack(results, 0)
```

```python
import math

import jax
import jax.numpy as jnp
import ml_dtypes
import numpy as np
from jax import lax
from jax.experimental import pallas as pl
from jax.experimental.pallas import tpu as pltpu
from jax.sharding import PartitionSpec as P

RAD_D = 3
RAD_S = 12
SIGMA_DERIV = 1.0
SIGMA_SMOOTH = 4.0

NB = 32
LANES = 128
HALO_SLOT = 16
MSG_ROWS = 72
F32 = jnp.float32
BF16 = jnp.bfloat16


def kernel_taps(radius, width_sigma, derivative):
    offsets = [float(t) for t in range(-radius, radius + 1)]
    weights = [math.exp(-0.5 * (t / width_sigma) ** 2) for t in offsets]
    if derivative:
        total = sum((t * t * w for t, w in zip(offsets, weights)))
        return [t * w / total for t, w in zip(offsets, weights)]
    total = sum(weights)
    return [w / total for w in weights]


G1 = kernel_taps(RAD_D, SIGMA_DERIV, False)
D1 = kernel_taps(RAD_D, SIGMA_DERIV, True)
G4 = kernel_taps(RAD_S, SIGMA_SMOOTH, False)


def halves(matrix):
    high = matrix.astype(ml_dtypes.bfloat16)
    low = (matrix - high.astype(np.float64)).astype(ml_dtypes.bfloat16)
    return high, low


def band(taps, n):
    radius = len(taps) // 2
    m = np.zeros((n, n))
    for i in range(n):
        for t in range(-radius, radius + 1):
            if 0 <= i + t < n:
                m[i, i + t] = taps[t + radius]
    return m


def y_gradient_matrix():
    m = np.zeros((2 * LANES, 2 * LANES))
    for part, taps in enumerate((G1, D1)):
        for y in range(LANES):
            for t in range(-RAD_D, RAD_D + 1):
                s = y + t
                w = taps[t + RAD_D]
                col = part * LANES + y
                if 0 <= s < LANES:
                    m[s, col] = w
                else:
                    k = s + RAD_D if s < 0 else RAD_D + s - LANES
                    for seg in range(8):
                        m[LANES + seg * HALO_SLOT + k, col] = w
    return m


def pair_order():
    return [(xp, 4 * d + z) for d in range(NB) for xp in range(2) for z in range(4)]


def z_gradient_matrix():
    smooth, deriv = band(G1, 128), band(D1, 128)
    m = np.zeros((512, 256))
    for col, (xp, z) in enumerate(pair_order()):
        m[xp * 128 : xp * 128 + 128, col] = smooth[:, z]
        m[256 + xp * 128 : 256 + xp * 128 + 128, col] = deriv[:, z]
    return m


def z_smooth_matrix():
    smooth = band(G4, 128)
    m = np.zeros((256, 256))
    for row, (xp, z) in enumerate(pair_order()):
        m[row, xp * 128 : xp * 128 + 128] = smooth[z]
    return m


def y_smooth_matrix():
    m = np.zeros((384, 256))
    for y in range(256):
        for t in range(-RAD_S, RAD_S + 1):
            s = y + t
            if s < 0:
                s = 256 + 128 + s
            elif s >= 256:
                s = 256 + s - 256
            m[s, y] = G4[t + RAD_S]
    return m


def split(x):
    high = x.astype(BF16)
    return high, (x - high.astype(F32)).astype(BF16)


def dot(a, b):
    return jnp.dot(a, b, preferred_element_type=F32)


def pack_kernel(occ_ref, vol_ref, out_ref):
    lane = lax.broadcasted_iota(jnp.int32, (8, LANES), 1)
    for p in range(8):
        present = occ_ref[p // 4, 0].astype(F32)
        rows = jnp.concatenate([vol_ref[2 * p], vol_ref[2 * p + 1]], axis=0) * present
        blocks = [rows[:, j * LANES : (j + 1) * LANES] for j in range(NB)]
        zero = jnp.zeros((8, LANES), F32)
        for j in range(NB):
            out_ref[j, 8 * p : 8 * p + 8, :] = blocks[j]
            before = blocks[j - 1] if j > 0 else zero
            after = blocks[j + 1] if j < NB - 1 else zero
            rim = jnp.where(lane >= LANES - 3, before, jnp.where(lane < 3, after, 0.0))
            rim = pltpu.roll(rim, 3, 1, stride=HALO_SLOT, stride_axis=0)
            out_ref[j, 64 + p, :] = jnp.sum(rim, axis=0)


def pack(volume, occupancy):
    return pl.pallas_call(
        pack_kernel,
        out_shape=jax.ShapeDtypeStruct((NB, MSG_ROWS, LANES), F32),
        in_specs=[
            pl.BlockSpec(memory_space=pltpu.SMEM),
            pl.BlockSpec(memory_space=pltpu.VMEM),
        ],
        out_specs=pl.BlockSpec(memory_space=pltpu.VMEM),
        name="pack",
    )(occupancy, volume)


NROW = 48
PROWS = 40


def tensor_kernel(
    edge_ref, left_ref, own_ref, right_ref, gh_ref, gl_ref, wh_ref, wl_ref, bh_ref, bl_ref,
    out_ref, fields, prods, sums,
):
    row = lax.broadcasted_iota(jnp.int32, (8, LANES), 0)
    lane = lax.broadcasted_iota(jnp.int32, (8, LANES), 1)
    mine = (row == lane // HALO_SLOT)[None]

    for part, src in enumerate((left_ref, own_ref, right_ref)):

        def pair(p, carry, part=part, src=src):
            first = pl.multiple_of(8 * p, 8)
            main = src[:, pl.ds(first, 8), :].reshape(256, LANES)
            rim = src[:, pl.ds(64 + p, 1), :]
            rim = jnp.where(mine, jnp.broadcast_to(rim, (NB, 8, LANES)), 0.0)
            xh, xl = split(jnp.concatenate([main, rim.reshape(256, LANES)], axis=1))
            y = dot(xh, gh_ref[...]) + dot(xl, gh_ref[...]) + dot(xh, gl_ref[...])
            yh, yl = split(y)
            smooth = (
                dot(wh_ref[:256, :], yh) + dot(wh_ref[:256, :], yl) + dot(wl_ref[:256, :], yh)
            )
            ah, al = yh[:, :LANES], yl[:, :LANES]
            deriv = dot(wh_ref[256:, :], ah) + dot(wh_ref[256:, :], al) + dot(wl_ref[256:, :], ah)
            e = 16 * part + 2 * p
            fields[0, pl.ds(e, 2)] = smooth[:, :LANES].reshape(2, 128, LANES)
            fields[1, pl.ds(e, 2)] = smooth[:, LANES:].reshape(2, 128, LANES)
            fields[2, pl.ds(e, 2)] = deriv.reshape(2, 128, LANES)
            return carry

        lax.fori_loop(0, 8, pair, 0)

    def product_row(r, carry):
        keep = jnp.where((r < 12) & (edge_ref[0] == 0), 0.0, 1.0)
        keep = jnp.where((r >= 28) & (edge_ref[0] == 3), 0.0, keep)
        for zt in range(16):
            rows = pl.ds(8 * zt, 8)

            def tap(f, t):
                return fields[f, r + (4 + t), rows, :]

            def sym(f):
                s = G1[3] * tap(f, 0)
                for t in (1, 2, 3):
                    s = s + G1[3 + t] * (tap(f, t) + tap(f, -t))
                return s * keep

            gx = D1[4] * (tap(0, 1) - tap(0, -1))
            for t in (2, 3):
                gx = gx + D1[3 + t] * (tap(0, t) - tap(0, -t))
            gx = gx * keep
            gy = sym(1)
            gz = sym(2)
            prods[0, r, rows, :] = gx * gx
            prods[1, r, rows, :] = gx * gy
            prods[2, r, rows, :] = gx * gz
            prods[3, r, rows, :] = gy * gy
            prods[4, r, rows, :] = gy * gz
            prods[5, r, rows, :] = gz * gz
        return carry

    lax.fori_loop(0, PROWS, product_row, 0)

    def smooth_x(i, carry):
        c = i // 16
        rows = pl.ds(pl.multiple_of(8 * (i % 16), 8), 8)
        col = [prods[c, r, rows, :] for r in range(PROWS)]
        for x in range(16):
            s = G4[12] * col[x + 12]
            for t in range(1, RAD_S + 1):
                s = s + G4[12 + t] * (col[x + 12 + t] + col[x + 12 - t])
            sums[c, x, rows, :] = s
        return carry

    lax.fori_loop(0, 96, smooth_x, 0)

    def smooth_z(i, carry):
        c = i // 4
        x = 4 * (i % 4)
        a = sums[c, pl.ds(x, 2)].reshape(256, LANES)
        b = sums[c, pl.ds(x + 2, 2)].reshape(256, LANES)
        sh, sl = split(jnp.concatenate([a, b], axis=1))
        o = dot(bh_ref[...], sh) + dot(bh_ref[...], sl) + dot(bl_ref[...], sh)
        first = pl.multiple_of(16 * i, 8)
        out_ref[:, pl.ds(first, 8), :] = o[:, :LANES].reshape(NB, 8, LANES)
        out_ref[:, pl.ds(first + 8, 8), :] = o[:, LANES:].reshape(NB, 8, LANES)
        return carry

    lax.fori_loop(0, 24, smooth_z, 0)


def tensor(place, left, own, right):
    gh, gl = halves(y_gradient_matrix())
    wh, wl = halves(z_gradient_matrix())
    bh, bl = halves(z_smooth_matrix())
    vmem = pl.BlockSpec(memory_space=pltpu.VMEM)
    return pl.pallas_call(
        tensor_kernel,
        out_shape=jax.ShapeDtypeStruct((NB, 384, LANES), F32),
        in_specs=[pl.BlockSpec(memory_space=pltpu.SMEM)] + [vmem] * 9,
        out_specs=vmem,
        scratch_shapes=[
            pltpu.VMEM((3, NROW, 128, LANES), F32),
            pltpu.VMEM((6, PROWS, 128, LANES), F32),
            pltpu.VMEM((6, 16, 128, LANES), F32),
        ],
        compiler_params=pltpu.CompilerParams(vmem_limit_bytes=60 * 2**20),
        name="tensor",
    )(place, left, own, right, *(jnp.asarray(m) for m in (gh, gl, wh, wl, bh, bl)))


def smooth_y_kernel(in_ref, mh_ref, ml_ref, out_ref):
    lane = lax.broadcasted_iota(jnp.int32, (64, LANES), 1)
    zero = jnp.zeros((64, LANES), F32)
    for j in range(0, NB, 2):
        before = in_ref[j - 1] if j > 0 else zero
        after = in_ref[j + 2] if j + 2 < NB else zero
        rims = jnp.where(lane < 64, after, before)
        xh, xl = split(jnp.concatenate([in_ref[j], in_ref[j + 1], rims], axis=1))
        o = dot(xh, mh_ref[...]) + dot(xl, mh_ref[...]) + dot(xh, ml_ref[...])
        for x in range(16):
            out_ref[0, x, :, 128 * j : 128 * j + 256] = o[4 * x : 4 * x + 4, :]


def smooth_y(received):
    mh, ml = halves(y_smooth_matrix())
    whole = pl.BlockSpec((384, 256), lambda c: (0, 0))
    return pl.pallas_call(
        smooth_y_kernel,
        grid=(6,),
        out_shape=jax.ShapeDtypeStruct((6, 16, 4, NB * LANES), F32),
        in_specs=[pl.BlockSpec((NB, 64, LANES), lambda c: (0, c, 0)), whole, whole],
        out_specs=pl.BlockSpec((1, 16, 4, NB * LANES), lambda c: (c, 0, 0, 0)),
        compiler_params=pltpu.CompilerParams(vmem_limit_bytes=40 * 2**20),
        name="smooth_y",
    )(received, jnp.asarray(mh), jnp.asarray(ml))


def on_device(volume, occupancy):
    message = pack(volume, occupancy)
    columns = lax.all_to_all(message, "dev", 0, 0, tiled=True)
    size = lax.axis_size("gx")
    up = [(i, i + 1) for i in range(size - 1)]
    down = [(i + 1, i) for i in range(size - 1)]
    left = lax.ppermute(columns, "gx", up)
    right = lax.ppermute(columns, "gx", down)
    place = lax.axis_index("gx").reshape(1)
    blocks = tensor(place, left, columns, right)
    received = lax.all_to_all(blocks, "dev", 0, 0, tiled=True)
    return smooth_y(received)


def solution(mesh):
    return jax.shard_map(
        on_device,
        mesh=mesh,
        in_specs=(P("gx", "dev", None), P("gx", "dev")),
        out_specs=P(None, "gx", "dev", None),
        check_vma=False,
    )
```

```python
import math

import jax
import jax.numpy as jnp
import ml_dtypes
import numpy as np
from jax import lax
from jax.experimental import pallas as pl
from jax.experimental.pallas import tpu as pltpu
from jax.sharding import PartitionSpec as P

RAD_D = 3
RAD_S = 12
SIGMA_DERIV = 1.0
SIGMA_SMOOTH = 4.0

NB = 32
LANES = 128
HALO_SLOT = 16
MSG_ROWS = 72
F32 = jnp.float32
BF16 = jnp.bfloat16


def kernel_taps(radius, width_sigma, derivative):
    offsets = [float(t) for t in range(-radius, radius + 1)]
    weights = [math.exp(-0.5 * (t / width_sigma) ** 2) for t in offsets]
    if derivative:
        total = sum((t * t * w for t, w in zip(offsets, weights)))
        return [t * w / total for t, w in zip(offsets, weights)]
    total = sum(weights)
    return [w / total for w in weights]


G1 = kernel_taps(RAD_D, SIGMA_DERIV, False)
D1 = kernel_taps(RAD_D, SIGMA_DERIV, True)
G4 = kernel_taps(RAD_S, SIGMA_SMOOTH, False)


def halves(matrix):
    high = matrix.astype(ml_dtypes.bfloat16)
    low = (matrix - high.astype(np.float64)).astype(ml_dtypes.bfloat16)
    return high, low


def band(taps, n):
    radius = len(taps) // 2
    m = np.zeros((n, n))
    for i in range(n):
        for t in range(-radius, radius + 1):
            if 0 <= i + t < n:
                m[i, i + t] = taps[t + radius]
    return m


def y_gradient_matrix():
    m = np.zeros((2 * LANES, 2 * LANES))
    for part, taps in enumerate((G1, D1)):
        for y in range(LANES):
            for t in range(-RAD_D, RAD_D + 1):
                s = y + t
                w = taps[t + RAD_D]
                col = part * LANES + y
                if 0 <= s < LANES:
                    m[s, col] = w
                else:
                    k = s + RAD_D if s < 0 else RAD_D + s - LANES
                    for seg in range(8):
                        m[LANES + seg * HALO_SLOT + k, col] = w
    return m


def pair_order():
    return [(xp, 4 * d + z) for d in range(NB) for xp in range(2) for z in range(4)]


def z_gradient_matrix():
    return np.concatenate([band(G1, 128), band(D1, 128)], axis=0)


def z_smooth_matrix():
    smooth = band(G4, 128)
    m = np.zeros((256, 256))
    for row, (xp, z) in enumerate(pair_order()):
        m[row, xp * 128 : xp * 128 + 128] = smooth[z]
    return m


def y_smooth_matrix():
    m = np.zeros((384, 256))
    for y in range(256):
        for t in range(-RAD_S, RAD_S + 1):
            s = y + t
            if s < 0:
                s = 256 + 128 + s
            elif s >= 256:
                s = 256 + s - 256
            m[s, y] = G4[t + RAD_S]
    return m


def split(x):
    high = x.astype(BF16)
    return high, (x - high.astype(F32)).astype(BF16)


def dot(a, b):
    return jnp.dot(a, b, preferred_element_type=F32)


def pack_kernel(occ_ref, vol_ref, out_ref):
    lane = lax.broadcasted_iota(jnp.int32, (8, LANES), 1)
    for p in range(8):
        present = occ_ref[0, p // 4].astype(F32)
        rows = jnp.concatenate([vol_ref[2 * p], vol_ref[2 * p + 1]], axis=0) * present
        blocks = [rows[:, j * LANES : (j + 1) * LANES] for j in range(NB)]
        zero = jnp.zeros((8, LANES), F32)
        for j in range(NB):
            out_ref[j, 8 * p : 8 * p + 8, :] = blocks[j]
            before = blocks[j - 1] if j > 0 else zero
            after = blocks[j + 1] if j < NB - 1 else zero
            rim = jnp.where(lane >= LANES - 3, before, jnp.where(lane < 3, after, 0.0))
            rim = pltpu.roll(rim, 3, 1, stride=HALO_SLOT, stride_axis=0)
            out_ref[j, 64 + p, :] = jnp.sum(rim, axis=0)


def pack(volume, occupancy):
    return pl.pallas_call(
        pack_kernel,
        out_shape=jax.ShapeDtypeStruct((NB, MSG_ROWS, LANES), F32),
        in_specs=[
            pl.BlockSpec(memory_space=pltpu.SMEM),
            pl.BlockSpec(memory_space=pltpu.VMEM),
        ],
        out_specs=pl.BlockSpec(memory_space=pltpu.VMEM),
        name="pack",
    )(occupancy.T, volume)


NROW = 48
PROWS = 40
BLOCKS_OUT = pltpu.VMEM
CHUNKS = ((0, 1, 2, 3, 4, 5),)


def smooth_products(chunk, grads, b_ref, out_ref, sums):
    def along_x(step):
        k = step // 4
        c = chunk[0] + k
        first = (c > 2).astype(jnp.int32) + (c > 4).astype(jnp.int32)
        second = c - 2 * (c > 2).astype(jnp.int32) - (c > 4).astype(jnp.int32)
        for q in range(4):
            rows = pl.ds(pl.multiple_of(32 * (step % 4) + 8 * q, 8), 8)
            col = [grads[first, r, rows, :] * grads[second, r, rows, :] for r in range(PROWS)]
            for x in range(16):
                s = G4[12] * col[x + 12]
                for t in range(1, RAD_S + 1):
                    s = s + G4[12 + t] * (col[x + 12 + t] + col[x + 12 - t])
                sums[k % 2, x, rows, :] = s

    def along_depth(step):
        k, x = step // 4, 4 * (step % 4)
        a = sums[k % 2, pl.ds(x, 2)].reshape(256, LANES)
        b = sums[k % 2, pl.ds(x + 2, 2)].reshape(256, LANES)
        sh, sl = split(jnp.concatenate([a, b], axis=1))
        o = dot(b_ref[...], jnp.concatenate([sh, sl, sh], axis=0))
        first = pl.multiple_of(16 * step, 16)
        out_ref[:, pl.ds(first, 8), :] = o[:, :LANES].reshape(NB, 8, LANES)
        out_ref[:, pl.ds(first + 8, 8), :] = o[:, LANES:].reshape(NB, 8, LANES)

    def end(step, carry):
        along_depth(step)
        return carry

    def begin(step, carry):
        along_x(step)
        return carry

    for k in range(len(chunk)):
        lax.fori_loop(4 * k, 4 * k + 4, begin, 0)
        lax.fori_loop(4 * k, 4 * k + 4, end, 0, unroll=4)


def gradient_kernel(
    place_ref, own_ref, partner_ref, cross_ref, g_ref, w_ref, b_ref, out_ref, *refs
):
    if len(CHUNKS) > 1:
        kept_ref, fields, grads, sums, sem = refs
    else:
        fields, grads, sums = refs
    place = place_ref[0]
    odd = place % 2
    row = lax.broadcasted_iota(jnp.int32, (8, LANES), 0)
    lane = lax.broadcasted_iota(jnp.int32, (8, LANES), 1)
    mine = (row == lane // HALO_SLOT)[None]

    bases = (16, 32 - 32 * odd, 32 * odd)
    for base, src in zip(bases, (own_ref, partner_ref, cross_ref)):

        def pair(p, carry, base=base, src=src):
            first = pl.multiple_of(8 * p, 8)
            main = src[:, pl.ds(first, 8), :]
            rim = src[:, pl.ds(64 + p, 1), :]
            rim = jnp.where(mine, jnp.broadcast_to(rim, (NB, 8, LANES)), 0.0)
            rows = [main[:, :4].reshape(128, LANES), main[:, 4:].reshape(128, LANES)]
            rims = [rim[:, :4].reshape(128, LANES), rim[:, 4:].reshape(128, LANES)]
            both = jnp.concatenate(
                [jnp.concatenate(rows, axis=0), jnp.concatenate(rims, axis=0)], axis=1
            )
            xh, xl = split(both)
            y = dot(jnp.concatenate([xh, xl, xh], axis=1), g_ref[...])
            yh, yl = split(y)

            def lanes(m, k):
                k = k * LANES
                return jnp.concatenate([m[:128, k : k + LANES], m[128:, k : k + LANES]], axis=1)

            sh, sl = lanes(yh, 0), lanes(yl, 0)
            dh, dl = lanes(yh, 1), lanes(yl, 1)
            both = dot(w_ref[...], jnp.concatenate([sh, sl, sh], axis=0))
            other = dot(w_ref[:128, :], jnp.concatenate([dh, dl, dh], axis=0))
            e = base + 2 * p
            for k in range(2):
                cols = slice(k * LANES, (k + 1) * LANES)
                fields[0, e + k] = both[:128, cols]
                fields[1, e + k] = other[:, cols]
                fields[2, e + k] = both[128:, cols]
            return carry

        lax.fori_loop(0, 8, pair, 0, unroll=8)

    def gradient_row(r, carry):
        keep = jnp.where((r < 12) & (place == 0), 0.0, 1.0)
        keep = jnp.where((r >= 28) & (place == 3), 0.0, keep)
        for zt in range(16):
            rows = pl.ds(8 * zt, 8)

            def tap(f, t):
                return fields[f, r + (4 + t), rows, :]

            def sym(f):
                s = G1[3] * tap(f, 0)
                for t in (1, 2, 3):
                    s = s + G1[3 + t] * (tap(f, t) + tap(f, -t))
                return s * keep

            gx = D1[4] * (tap(0, 1) - tap(0, -1))
            for t in (2, 3):
                gx = gx + D1[3 + t] * (tap(0, t) - tap(0, -t))
            grads[0, r, rows, :] = gx * keep
            grads[1, r, rows, :] = sym(1)
            grads[2, r, rows, :] = sym(2)
        return carry

    lax.fori_loop(0, PROWS, gradient_row, 0, unroll=2)

    if len(CHUNKS) > 1:
        keep = pltpu.make_async_copy(grads, kept_ref, sem)
        keep.start()
    smooth_products(CHUNKS[0], grads, b_ref, out_ref, sums)
    if len(CHUNKS) > 1:
        keep.wait()


def product_kernel(chunk, grads, b_ref, out_ref, sums):
    smooth_products(chunk, grads, b_ref, out_ref, sums)


VMEM = pl.BlockSpec(memory_space=pltpu.VMEM)
FIELDS = (3, PROWS, 128, LANES)
SUMS = pltpu.VMEM((2, 16, 128, LANES), F32)


def gradients(place, own, partner, cross):
    gh, gl = halves(y_gradient_matrix())
    wh, wl = halves(z_gradient_matrix())
    g = np.concatenate([gh, gh, gl], axis=0)
    w = np.concatenate([wh, wh, wl], axis=1)
    blocks = (NB, 64 * len(CHUNKS[0]), LANES)
    scratch = [pltpu.VMEM((3, NROW, 128, LANES), F32), pltpu.VMEM(FIELDS, F32), SUMS]
    if len(CHUNKS) > 1:
        out_shape = (pltpu.HBM(blocks, F32), pltpu.HBM(FIELDS, F32))
        out_specs = (VMEM, pl.BlockSpec(memory_space=pl.ANY))
        scratch.append(pltpu.SemaphoreType.DMA)
    else:
        out_shape, out_specs = (BLOCKS_OUT(blocks, F32),), (VMEM,)
    return pl.pallas_call(
        gradient_kernel,
        out_shape=out_shape,
        in_specs=[pl.BlockSpec(memory_space=pltpu.SMEM)] + [VMEM] * 6,
        out_specs=out_specs,
        scratch_shapes=scratch,
        compiler_params=pltpu.CompilerParams(vmem_limit_bytes=36 * 2**20),
        cost_estimate=pl.CostEstimate(flops=10**10, transcendentals=0, bytes_accessed=2 * 10**7),
        name="gradients",
    )(place, own, partner, cross, in_hbm(g), in_hbm(w), smooth_matrix())


def in_hbm(m):
    return pltpu.with_memory_space_constraint(jnp.asarray(m), pltpu.HBM)


def smooth_matrix():
    bh, bl = halves(z_smooth_matrix())
    return in_hbm(np.concatenate([bh, bh, bl], axis=1))


def smoothed_products(grads, chunk):
    return pl.pallas_call(
        lambda *refs: product_kernel(chunk, *refs),
        out_shape=pltpu.HBM((NB, 64 * len(chunk), LANES), F32),
        in_specs=[VMEM, VMEM],
        out_specs=VMEM,
        scratch_shapes=[SUMS],
        compiler_params=pltpu.CompilerParams(vmem_limit_bytes=24 * 2**20),
        cost_estimate=pl.CostEstimate(flops=10**10, transcendentals=0, bytes_accessed=2 * 10**7),
        name="products",
    )(grads, smooth_matrix())


GROUP = 8


def smooth_y_kernel(in_ref, m_ref, *refs):
    out_ref = refs[-1]
    lane = lax.broadcasted_iota(jnp.int32, (64, LANES), 1)
    zero = jnp.zeros((64, LANES), F32)
    for start in range(0, NB, 2 * GROUP):
        stack = []
        for j in range(start, start + 2 * GROUP, 2):
            before = in_ref[j - 1] if j > 0 else zero
            after = in_ref[j + 2] if j + 2 < NB else zero
            rims = jnp.where(lane < 64, after, before)
            xh, xl = split(jnp.concatenate([in_ref[j], in_ref[j + 1], rims], axis=1))
            stack.append(jnp.concatenate([xh, xl, xh], axis=1))
        o = dot(jnp.concatenate(stack, axis=0), m_ref[...])
        for k in range(GROUP):
            j = start + 2 * k
            for x in range(16):
                first = 64 * k + 4 * x
                out_ref[0, x, :, 128 * j : 128 * j + 256] = o[first : first + 4, :]


def smooth_y(received, where, out):
    mh, ml = halves(y_smooth_matrix())
    m = in_hbm(np.concatenate([mh, mh, ml], axis=0))
    first = where[0]
    args = [received, m] + ([] if out is None else [out])
    return pl.pallas_call(
        smooth_y_kernel,
        grid=(len(where),),
        out_shape=jax.ShapeDtypeStruct((6, 16, 4, NB * LANES), F32),
        in_specs=[pl.BlockSpec((NB, 64, LANES), lambda c: (0, c, 0)), VMEM]
        + [pl.BlockSpec(memory_space=pl.ANY)] * (len(args) - 2),
        out_specs=pl.BlockSpec((1, 16, 4, NB * LANES), lambda c: (first + c, 0, 0, 0)),
        input_output_aliases={} if out is None else {2: 0},
        compiler_params=pltpu.CompilerParams(vmem_limit_bytes=24 * 2**20),
        cost_estimate=pl.CostEstimate(flops=6 * 10**9, transcendentals=0, bytes_accessed=10**7),
        name="smooth_y",
    )(*args)


def on_device(volume, occupancy):
    message = pack(volume, occupancy)
    columns = lax.all_to_all(message, "dev", 0, 0, tiled=True)
    partner = lax.ppermute(columns, "gx", [(0, 1), (1, 0), (2, 3), (3, 2)])
    cross = lax.ppermute(columns, "gx", [(1, 2), (2, 1)])
    place = lax.axis_index("gx").reshape(1)
    blocks, *grads = gradients(place, columns, partner, cross)
    received = [lax.all_to_all(blocks, "dev", 0, 0, tiled=True)]
    for chunk in CHUNKS[1:]:
        blocks = smoothed_products(grads[0], chunk)
        received.append(lax.all_to_all(blocks, "dev", 0, 0, tiled=True))
    out = None
    for chunk, part in zip(CHUNKS, received):
        out = smooth_y(part, chunk, out)
    return out


def solution(mesh):
    return jax.shard_map(
        on_device,
        mesh=mesh,
        in_specs=(P("gx", "dev", None), P("gx", "dev")),
        out_specs=P(None, "gx", "dev", None),
        check_vma=False,
    )
```

```python
import math

import jax
import jax.numpy as jnp
import ml_dtypes
import numpy as np
from jax import lax
from jax.experimental import pallas as pl
from jax.experimental.pallas import tpu as pltpu
from jax.sharding import PartitionSpec as P

RAD_D = 3
RAD_S = 12
SIGMA_DERIV = 1.0
SIGMA_SMOOTH = 4.0

NB = 32
LANES = 128
HALO_SLOT = 16
MSG_ROWS = 72
F32 = jnp.float32
BF16 = jnp.bfloat16


def kernel_taps(radius, width_sigma, derivative):
    offsets = [float(t) for t in range(-radius, radius + 1)]
    weights = [math.exp(-0.5 * (t / width_sigma) ** 2) for t in offsets]
    if derivative:
        total = sum((t * t * w for t, w in zip(offsets, weights)))
        return [t * w / total for t, w in zip(offsets, weights)]
    total = sum(weights)
    return [w / total for w in weights]


G1 = kernel_taps(RAD_D, SIGMA_DERIV, False)
D1 = kernel_taps(RAD_D, SIGMA_DERIV, True)
G4 = kernel_taps(RAD_S, SIGMA_SMOOTH, False)


def halves(matrix):
    high = matrix.astype(ml_dtypes.bfloat16)
    low = (matrix - high.astype(np.float64)).astype(ml_dtypes.bfloat16)
    return high, low


def band(taps, n):
    radius = len(taps) // 2
    m = np.zeros((n, n))
    for i in range(n):
        for t in range(-radius, radius + 1):
            if 0 <= i + t < n:
                m[i, i + t] = taps[t + radius]
    return m


def y_gradient_matrix():
    m = np.zeros((2 * LANES, 2 * LANES))
    for part, taps in enumerate((G1, D1)):
        for y in range(LANES):
            for t in range(-RAD_D, RAD_D + 1):
                s = y + t
                w = taps[t + RAD_D]
                col = part * LANES + y
                if 0 <= s < LANES:
                    m[s, col] = w
                else:
                    k = s + RAD_D if s < 0 else RAD_D + s - LANES
                    for seg in range(8):
                        m[LANES + seg * HALO_SLOT + k, col] = w
    return m


def pair_order():
    return [(xp, 4 * d + z) for d in range(NB) for xp in range(2) for z in range(4)]


def z_gradient_matrix():
    return np.concatenate([band(G1, 128), band(D1, 128)], axis=0)


def z_smooth_matrix():
    smooth = band(G4, 128)
    m = np.zeros((256, 256))
    for row, (xp, z) in enumerate(pair_order()):
        m[row, xp * 128 : xp * 128 + 128] = smooth[z]
    return m


def y_smooth_matrix():
    m = np.zeros((384, 256))
    for y in range(256):
        for t in range(-RAD_S, RAD_S + 1):
            s = y + t
            if s < 0:
                s = 256 + 128 + s
            elif s >= 256:
                s = 256 + s - 256
            m[s, y] = G4[t + RAD_S]
    return m


def split(x):
    high = x.astype(BF16)
    return high, (x - high.astype(F32)).astype(BF16)


def dot(a, b):
    return jnp.dot(a, b, preferred_element_type=F32)


def pack_kernel(occ_ref, vol_ref, out_ref):
    lane = lax.broadcasted_iota(jnp.int32, (8, LANES), 1)
    for p in range(8):
        present = occ_ref[0, p // 4].astype(F32)
        rows = jnp.concatenate([vol_ref[2 * p], vol_ref[2 * p + 1]], axis=0) * present
        blocks = [rows[:, j * LANES : (j + 1) * LANES] for j in range(NB)]
        zero = jnp.zeros((8, LANES), F32)
        for j in range(NB):
            out_ref[j, 8 * p : 8 * p + 8, :] = blocks[j]
            before = blocks[j - 1] if j > 0 else zero
            after = blocks[j + 1] if j < NB - 1 else zero
            rim = jnp.where(lane >= LANES - 3, before, jnp.where(lane < 3, after, 0.0))
            rim = pltpu.roll(rim, 3, 1, stride=HALO_SLOT, stride_axis=0)
            out_ref[j, 64 + p, :] = jnp.sum(rim, axis=0)


def pack(volume, occupancy):
    return pl.pallas_call(
        pack_kernel,
        out_shape=pltpu.VMEM((NB, MSG_ROWS, LANES), F32),
        in_specs=[
            pl.BlockSpec(memory_space=pltpu.SMEM),
            pl.BlockSpec(memory_space=pltpu.VMEM),
        ],
        out_specs=pl.BlockSpec(memory_space=pltpu.VMEM),
        name="pack",
    )(occupancy.T, volume)


NROW = 48
PROWS = 40


def smooth_products(chunk, grads, b_ref, out_ref, sums):
    def along_x(step):
        k = step // 4
        c = chunk[0] + k
        first = (c > 2).astype(jnp.int32) + (c > 4).astype(jnp.int32)
        second = c - 2 * (c > 2).astype(jnp.int32) - (c > 4).astype(jnp.int32)
        for q in range(4):
            rows = pl.ds(pl.multiple_of(32 * (step % 4) + 8 * q, 8), 8)
            col = [grads[first, r, rows, :] * grads[second, r, rows, :] for r in range(PROWS)]
            for x in range(16):
                s = G4[12] * col[x + 12]
                for t in range(1, RAD_S + 1):
                    s = s + G4[12 + t] * (col[x + 12 + t] + col[x + 12 - t])
                sums[k % 2, x, rows, :] = s

    def along_depth(step):
        k, x = step // 4, 4 * (step % 4)
        a = sums[k % 2, pl.ds(x, 2)].reshape(256, LANES)
        b = sums[k % 2, pl.ds(x + 2, 2)].reshape(256, LANES)
        sh, sl = split(jnp.concatenate([a, b], axis=1))
        o = dot(b_ref[...], jnp.concatenate([sh, sl, sh], axis=0))
        first = pl.multiple_of(16 * step, 16)
        out_ref[:, pl.ds(first, 8), :] = o[:, :LANES].reshape(NB, 8, LANES)
        out_ref[:, pl.ds(first + 8, 8), :] = o[:, LANES:].reshape(NB, 8, LANES)

    def end(step, carry):
        along_depth(step)
        return carry

    def begin(step, carry):
        along_x(step)
        return carry

    for k in range(len(chunk)):
        lax.fori_loop(4 * k, 4 * k + 4, begin, 0)
        lax.fori_loop(4 * k, 4 * k + 4, end, 0, unroll=4)


NEAR = 25
FAR = PROWS - NEAR
EDGE = 6


def line_fields(src, base, g_ref, w_ref, fields):
    row = lax.broadcasted_iota(jnp.int32, (8, LANES), 0)
    lane = lax.broadcasted_iota(jnp.int32, (8, LANES), 1)
    mine = (row == lane // HALO_SLOT)[None]

    def pair(p, carry):
        first = pl.multiple_of(8 * p, 8)
        main = src[:, pl.ds(first, 8), :]
        rim = src[:, pl.ds(64 + p, 1), :]
        rim = jnp.where(mine, jnp.broadcast_to(rim, (NB, 8, LANES)), 0.0)
        rows = [main[:, :4].reshape(128, LANES), main[:, 4:].reshape(128, LANES)]
        rims = [rim[:, :4].reshape(128, LANES), rim[:, 4:].reshape(128, LANES)]
        both = jnp.concatenate(
            [jnp.concatenate(rows, axis=0), jnp.concatenate(rims, axis=0)], axis=1
        )
        xh, xl = split(both)
        y = dot(jnp.concatenate([xh, xl, xh], axis=1), g_ref[...])
        yh, yl = split(y)

        def lanes(m, k):
            k = k * LANES
            return jnp.concatenate([m[:128, k : k + LANES], m[128:, k : k + LANES]], axis=1)

        sh, sl = lanes(yh, 0), lanes(yl, 0)
        dh, dl = lanes(yh, 1), lanes(yl, 1)
        both = dot(w_ref[...], jnp.concatenate([sh, sl, sh], axis=0))
        other = dot(w_ref[:128, :], jnp.concatenate([dh, dl, dh], axis=0))
        e = base + 2 * p
        for k in range(2):
            cols = slice(k * LANES, (k + 1) * LANES)
            fields[0, e + k] = both[:128, cols]
            fields[1, e + k] = other[:, cols]
            fields[2, e + k] = both[128:, cols]
        return carry

    lax.fori_loop(0, 8, pair, 0, unroll=8)


def gradient_rows(place, fields, start, count, out, out_start, unroll):
    def one(i, carry):
        r = start + i
        keep = jnp.where((r < 12) & (place == 0), 0.0, 1.0)
        keep = jnp.where((r >= 28) & (place == 3), 0.0, keep)
        for zt in range(16):
            rows = pl.ds(8 * zt, 8)

            def tap(f, t):
                return fields[f, r + (4 + t), rows, :]

            def sym(f):
                s = G1[3] * tap(f, 0)
                for t in (1, 2, 3):
                    s = s + G1[3 + t] * (tap(f, t) + tap(f, -t))
                return s * keep

            gx = D1[4] * (tap(0, 1) - tap(0, -1))
            for t in (2, 3):
                gx = gx + D1[3 + t] * (tap(0, t) - tap(0, -t))
            out[0, out_start + i, rows, :] = gx * keep
            out[1, out_start + i, rows, :] = sym(1)
            out[2, out_start + i, rows, :] = sym(2)
        return carry

    lax.fori_loop(0, count, one, 0, unroll=unroll)


def near_kernel(place_ref, own_ref, partner_ref, g_ref, w_ref, edge_ref, near_ref, fields):
    place = place_ref[0]
    odd = place % 2
    line_fields(own_ref, 16, g_ref, w_ref, fields)
    line_fields(partner_ref, 32 - 32 * odd, g_ref, w_ref, fields)
    for f in range(3):
        for k in range(EDGE):
            edge_ref[f, k] = fields[f, 16 + 10 * odd + k]
    gradient_rows(place, fields, FAR - FAR * odd, NEAR, near_ref, 0, 5)


def far_kernel(
    place_ref, cross_ref, edge_ref, near_ref, g_ref, w_ref, b_ref, out_ref, fields, grads, sums
):
    place = place_ref[0]
    odd = place % 2
    line_fields(cross_ref, 32 * odd, g_ref, w_ref, fields)
    for f in range(3):
        for k in range(EDGE):
            fields[f, 16 + 10 * odd + k] = edge_ref[f, k]
    far = NEAR * odd
    gradient_rows(place, fields, far, FAR, grads, far, 3)

    def copy(i, carry):
        for f in range(3):
            grads[f, FAR - FAR * odd + i] = near_ref[f, i]
        return carry

    lax.fori_loop(0, NEAR, copy, 0)
    smooth_products(range(6), grads, b_ref, out_ref, sums)


VMEM = pl.BlockSpec(memory_space=pltpu.VMEM)
SMEM = pl.BlockSpec(memory_space=pltpu.SMEM)
FIELDS = pltpu.VMEM((3, NROW, 128, LANES), F32)


def gradient_matrices():
    gh, gl = halves(y_gradient_matrix())
    wh, wl = halves(z_gradient_matrix())
    g = np.concatenate([gh, gh, gl], axis=0)
    w = np.concatenate([wh, wh, wl], axis=1)
    return in_hbm(g), in_hbm(w)


def near_gradients(place, own, partner):
    return pl.pallas_call(
        near_kernel,
        out_shape=(
            pltpu.VMEM((3, EDGE, 128, LANES), F32),
            pltpu.VMEM((3, NEAR, 128, LANES), F32),
        ),
        in_specs=[SMEM] + [VMEM] * 4,
        out_specs=(VMEM, VMEM),
        scratch_shapes=[FIELDS],
        compiler_params=pltpu.CompilerParams(vmem_limit_bytes=30 * 2**20),
        cost_estimate=pl.CostEstimate(flops=10**10, transcendentals=0, bytes_accessed=2 * 10**7),
        name="near",
    )(place, own, partner, *gradient_matrices())


def products(place, cross, edge, near):
    return pl.pallas_call(
        far_kernel,
        out_shape=pltpu.VMEM((NB, 384, LANES), F32),
        in_specs=[SMEM] + [VMEM] * 6,
        out_specs=VMEM,
        scratch_shapes=[
            FIELDS,
            pltpu.VMEM((3, PROWS, 128, LANES), F32),
            pltpu.VMEM((2, 16, 128, LANES), F32),
        ],
        compiler_params=pltpu.CompilerParams(vmem_limit_bytes=38 * 2**20),
        cost_estimate=pl.CostEstimate(flops=10**10, transcendentals=0, bytes_accessed=2 * 10**7),
        name="products",
    )(place, cross, edge, near, *gradient_matrices(), smooth_matrix())


def in_hbm(m):
    return pltpu.with_memory_space_constraint(jnp.asarray(m), pltpu.HBM)


def smooth_matrix():
    bh, bl = halves(z_smooth_matrix())
    return in_hbm(np.concatenate([bh, bh, bl], axis=1))


GROUP = 8


def smooth_y_kernel(in_ref, m_ref, out_ref):
    lane = lax.broadcasted_iota(jnp.int32, (64, LANES), 1)
    zero = jnp.zeros((64, LANES), F32)
    for start in range(0, NB, 2 * GROUP):
        stack = []
        for j in range(start, start + 2 * GROUP, 2):
            before = in_ref[j - 1] if j > 0 else zero
            after = in_ref[j + 2] if j + 2 < NB else zero
            rims = jnp.where(lane < 64, after, before)
            xh, xl = split(jnp.concatenate([in_ref[j], in_ref[j + 1], rims], axis=1))
            stack.append(jnp.concatenate([xh, xl, xh], axis=1))
        o = dot(jnp.concatenate(stack, axis=0), m_ref[...])
        for k in range(GROUP):
            j = start + 2 * k
            for x in range(16):
                first = 64 * k + 4 * x
                out_ref[0, x, :, 128 * j : 128 * j + 256] = o[first : first + 4, :]


def smooth_y(received):
    mh, ml = halves(y_smooth_matrix())
    m = in_hbm(np.concatenate([mh, mh, ml], axis=0))
    return pl.pallas_call(
        smooth_y_kernel,
        grid=(6,),
        out_shape=jax.ShapeDtypeStruct((6, 16, 4, NB * LANES), F32),
        in_specs=[pl.BlockSpec((NB, 64, LANES), lambda c: (0, c, 0)), VMEM],
        out_specs=pl.BlockSpec((1, 16, 4, NB * LANES), lambda c: (c, 0, 0, 0)),
        compiler_params=pltpu.CompilerParams(vmem_limit_bytes=24 * 2**20),
        cost_estimate=pl.CostEstimate(flops=6 * 10**9, transcendentals=0, bytes_accessed=10**7),
        name="smooth_y",
    )(received, m)


def on_device(volume, occupancy):
    message = pack(volume, occupancy)
    columns = lax.all_to_all(message, "dev", 0, 0, tiled=True)
    partner = lax.ppermute(columns, "gx", [(0, 1), (1, 0), (2, 3), (3, 2)])
    cross = lax.ppermute(columns, "gx", [(1, 2), (2, 1)])
    place = lax.axis_index("gx").reshape(1)
    edge, near = near_gradients(place, columns, partner)
    blocks = products(place, cross, edge, near)
    received = lax.all_to_all(blocks, "dev", 0, 0, tiled=True)
    return smooth_y(received)


def solution(mesh):
    return jax.shard_map(
        on_device,
        mesh=mesh,
        in_specs=(P("gx", "dev", None), P("gx", "dev")),
        out_specs=P(None, "gx", "dev", None),
        check_vma=False,
    )
```

```python
import math

import jax
import jax.numpy as jnp
import ml_dtypes
import numpy as np
from jax import lax
from jax.experimental import pallas as pl
from jax.experimental.pallas import tpu as pltpu
from jax.sharding import PartitionSpec as P

RAD_D = 3
RAD_S = 12
SIGMA_DERIV = 1.0
SIGMA_SMOOTH = 4.0

NB = 32
LANES = 128
HALO_SLOT = 16
MSG_ROWS = 72
F32 = jnp.float32
BF16 = jnp.bfloat16


def kernel_taps(radius, width_sigma, derivative):
    offsets = [float(t) for t in range(-radius, radius + 1)]
    weights = [math.exp(-0.5 * (t / width_sigma) ** 2) for t in offsets]
    if derivative:
        total = sum((t * t * w for t, w in zip(offsets, weights)))
        return [t * w / total for t, w in zip(offsets, weights)]
    total = sum(weights)
    return [w / total for w in weights]


G1 = kernel_taps(RAD_D, SIGMA_DERIV, False)
D1 = kernel_taps(RAD_D, SIGMA_DERIV, True)
G4 = kernel_taps(RAD_S, SIGMA_SMOOTH, False)


def halves(matrix):
    high = matrix.astype(ml_dtypes.bfloat16)
    low = (matrix - high.astype(np.float64)).astype(ml_dtypes.bfloat16)
    return high, low


def band(taps, n):
    radius = len(taps) // 2
    m = np.zeros((n, n))
    for i in range(n):
        for t in range(-radius, radius + 1):
            if 0 <= i + t < n:
                m[i, i + t] = taps[t + radius]
    return m


def y_gradient_matrix():
    m = np.zeros((2 * LANES, 2 * LANES))
    for part, taps in enumerate((G1, D1)):
        for y in range(LANES):
            for t in range(-RAD_D, RAD_D + 1):
                s = y + t
                w = taps[t + RAD_D]
                col = part * LANES + y
                if 0 <= s < LANES:
                    m[s, col] = w
                else:
                    k = s + RAD_D if s < 0 else RAD_D + s - LANES
                    for seg in range(8):
                        m[LANES + seg * HALO_SLOT + k, col] = w
    return m


def pair_order():
    return [(xp, 4 * d + z) for d in range(NB) for xp in range(2) for z in range(4)]


def z_gradient_matrix():
    return np.concatenate([band(G1, 128), band(D1, 128)], axis=0)


def z_smooth_matrix():
    smooth = band(G4, 128)
    m = np.zeros((256, 256))
    for row, (xp, z) in enumerate(pair_order()):
        m[row, xp * 128 : xp * 128 + 128] = smooth[z]
    return m


def y_smooth_matrix():
    m = np.zeros((384, 256))
    for y in range(256):
        for t in range(-RAD_S, RAD_S + 1):
            s = y + t
            if s < 0:
                s = 256 + 128 + s
            elif s >= 256:
                s = 256 + s - 256
            m[s, y] = G4[t + RAD_S]
    return m


def split(x):
    high = x.astype(BF16)
    return high, (x - high.astype(F32)).astype(BF16)


def dot(a, b):
    return jnp.dot(a, b, preferred_element_type=F32)


def pack_kernel(occ_ref, vol_ref, out_ref):
    lane = lax.broadcasted_iota(jnp.int32, (8, LANES), 1)
    for p in range(8):
        present = occ_ref[0, p // 4].astype(F32)
        rows = jnp.concatenate([vol_ref[2 * p], vol_ref[2 * p + 1]], axis=0) * present
        blocks = [rows[:, j * LANES : (j + 1) * LANES] for j in range(NB)]
        zero = jnp.zeros((8, LANES), F32)
        for j in range(NB):
            out_ref[j, 8 * p : 8 * p + 8, :] = blocks[j]
            before = blocks[j - 1] if j > 0 else zero
            after = blocks[j + 1] if j < NB - 1 else zero
            rim = jnp.where(lane >= LANES - 3, before, jnp.where(lane < 3, after, 0.0))
            rim = pltpu.roll(rim, 3, 1, stride=HALO_SLOT, stride_axis=0)
            out_ref[j, 64 + p, :] = jnp.sum(rim, axis=0)


def pack(volume, occupancy):
    return pl.pallas_call(
        pack_kernel,
        out_shape=pltpu.VMEM((NB, MSG_ROWS, LANES), F32),
        in_specs=[
            pl.BlockSpec(memory_space=pltpu.SMEM),
            pl.BlockSpec(memory_space=pltpu.VMEM),
        ],
        out_specs=pl.BlockSpec(memory_space=pltpu.VMEM),
        name="pack",
    )(occupancy.T, volume)


NROW = 48
PROWS = 40


def smooth_products(chunk, grads, b_ref, out_ref, sums):
    def along_x(step):
        k = step // 4
        c = chunk[0] + k
        first = (c > 2).astype(jnp.int32) + (c > 4).astype(jnp.int32)
        second = c - 2 * (c > 2).astype(jnp.int32) - (c > 4).astype(jnp.int32)
        for q in range(4):
            rows = pl.ds(pl.multiple_of(32 * (step % 4) + 8 * q, 8), 8)
            col = [grads[first, r, rows, :] * grads[second, r, rows, :] for r in range(PROWS)]
            for x in range(16):
                s = G4[12] * col[x + 12]
                for t in range(1, RAD_S + 1):
                    s = s + G4[12 + t] * (col[x + 12 + t] + col[x + 12 - t])
                sums[k % 2, x, rows, :] = s

    def along_depth(step):
        k, x = step // 4, 4 * (step % 4)
        a = sums[k % 2, pl.ds(x, 2)].reshape(256, LANES)
        b = sums[k % 2, pl.ds(x + 2, 2)].reshape(256, LANES)
        sh, sl = split(jnp.concatenate([a, b], axis=1))
        o = dot(b_ref[...], jnp.concatenate([sh, sl, sh], axis=0))
        first = pl.multiple_of(16 * step, 16)
        out_ref[:, pl.ds(first, 8), :] = o[:, :LANES].reshape(NB, 8, LANES)
        out_ref[:, pl.ds(first + 8, 8), :] = o[:, LANES:].reshape(NB, 8, LANES)

    def end(step, carry):
        along_depth(step)
        return carry

    def begin(step, carry):
        along_x(step)
        return carry

    for k in range(len(chunk)):
        lax.fori_loop(4 * k, 4 * k + 4, begin, 0)
        lax.fori_loop(4 * k, 4 * k + 4, end, 0, unroll=4)


NEAR = 25
FAR = PROWS - NEAR
EDGE = 6


def line_fields(src, base, g_ref, w_ref, fields):
    row = lax.broadcasted_iota(jnp.int32, (8, LANES), 0)
    lane = lax.broadcasted_iota(jnp.int32, (8, LANES), 1)
    mine = (row == lane // HALO_SLOT)[None]

    def pair(p, carry):
        first = pl.multiple_of(8 * p, 8)
        main = src[:, pl.ds(first, 8), :]
        rim = src[:, pl.ds(64 + p, 1), :]
        rim = jnp.where(mine, jnp.broadcast_to(rim, (NB, 8, LANES)), 0.0)
        rows = [main[:, :4].reshape(128, LANES), main[:, 4:].reshape(128, LANES)]
        rims = [rim[:, :4].reshape(128, LANES), rim[:, 4:].reshape(128, LANES)]
        both = jnp.concatenate(
            [jnp.concatenate(rows, axis=0), jnp.concatenate(rims, axis=0)], axis=1
        )
        xh, xl = split(both)
        y = dot(jnp.concatenate([xh, xl, xh], axis=1), g_ref[...])
        yh, yl = split(y)

        def lanes(m, k):
            k = k * LANES
            return jnp.concatenate([m[:128, k : k + LANES], m[128:, k : k + LANES]], axis=1)

        sh, sl = lanes(yh, 0), lanes(yl, 0)
        dh, dl = lanes(yh, 1), lanes(yl, 1)
        both = dot(w_ref[...], jnp.concatenate([sh, sl, sh], axis=0))
        other = dot(w_ref[:128, :], jnp.concatenate([dh, dl, dh], axis=0))
        e = base + 2 * p
        for k in range(2):
            cols = slice(k * LANES, (k + 1) * LANES)
            fields[0, e + k] = both[:128, cols]
            fields[1, e + k] = other[:, cols]
            fields[2, e + k] = both[128:, cols]
        return carry

    lax.fori_loop(0, 8, pair, 0, unroll=8)


def gradient_rows(place, fields, start, count, out, out_start, unroll):
    def one(i, carry):
        r = start + i
        keep = jnp.where((r < 12) & (place == 0), 0.0, 1.0)
        keep = jnp.where((r >= 28) & (place == 3), 0.0, keep)
        for zt in range(16):
            rows = pl.ds(8 * zt, 8)

            def tap(f, t):
                return fields[f, r + (4 + t), rows, :]

            def sym(f):
                s = G1[3] * tap(f, 0)
                for t in (1, 2, 3):
                    s = s + G1[3 + t] * (tap(f, t) + tap(f, -t))
                return s * keep

            gx = D1[4] * (tap(0, 1) - tap(0, -1))
            for t in (2, 3):
                gx = gx + D1[3 + t] * (tap(0, t) - tap(0, -t))
            out[0, out_start + i, rows, :] = gx * keep
            out[1, out_start + i, rows, :] = sym(1)
            out[2, out_start + i, rows, :] = sym(2)
        return carry

    lax.fori_loop(0, count, one, 0, unroll=unroll)


def near_kernel(place_ref, own_ref, partner_ref, g_ref, w_ref, edge_ref, near_ref, fields):
    place = place_ref[0]
    odd = place % 2
    line_fields(own_ref, 16, g_ref, w_ref, fields)
    line_fields(partner_ref, 32 - 32 * odd, g_ref, w_ref, fields)
    for f in range(3):
        for k in range(EDGE):
            edge_ref[f, k] = fields[f, 16 + 10 * odd + k]
    gradient_rows(place, fields, FAR - FAR * odd, NEAR, near_ref, 0, 5)


def far_kernel(
    place_ref, cross_ref, edge_ref, near_ref, g_ref, w_ref, b_ref, out_ref, fields, grads, sums
):
    place = place_ref[0]
    odd = place % 2
    line_fields(cross_ref, 32 * odd, g_ref, w_ref, fields)
    for f in range(3):
        for k in range(EDGE):
            fields[f, 16 + 10 * odd + k] = edge_ref[f, k]
    far = NEAR * odd
    gradient_rows(place, fields, far, FAR, grads, far, 3)

    def copy(i, carry):
        for f in range(3):
            grads[f, FAR - FAR * odd + i] = near_ref[f, i]
        return carry

    lax.fori_loop(0, NEAR, copy, 0)
    smooth_products(range(6), grads, b_ref, out_ref, sums)


VMEM = pl.BlockSpec(memory_space=pltpu.VMEM)
SMEM = pl.BlockSpec(memory_space=pltpu.SMEM)
FIELDS = pltpu.VMEM((3, NROW, 128, LANES), F32)


def gradient_matrices():
    gh, gl = halves(y_gradient_matrix())
    wh, wl = halves(z_gradient_matrix())
    g = np.concatenate([gh, gh, gl], axis=0)
    w = np.concatenate([wh, wh, wl], axis=1)
    return in_hbm(g), in_hbm(w)


def near_gradients(place, own, partner):
    return pl.pallas_call(
        near_kernel,
        out_shape=(
            pltpu.VMEM((3, EDGE, 128, LANES), F32),
            pltpu.VMEM((3, NEAR, 128, LANES), F32),
        ),
        in_specs=[SMEM] + [VMEM] * 4,
        out_specs=(VMEM, VMEM),
        scratch_shapes=[FIELDS],
        compiler_params=pltpu.CompilerParams(vmem_limit_bytes=30 * 2**20),
        cost_estimate=pl.CostEstimate(flops=10**10, transcendentals=0, bytes_accessed=2 * 10**7),
        name="near",
    )(place, own, partner, *gradient_matrices())


def products(place, cross, edge, near):
    return pl.pallas_call(
        far_kernel,
        out_shape=pltpu.VMEM((NB, 384, LANES), F32),
        in_specs=[SMEM] + [VMEM] * 6,
        out_specs=VMEM,
        scratch_shapes=[
            FIELDS,
            pltpu.VMEM((3, PROWS, 128, LANES), F32),
            pltpu.VMEM((2, 16, 128, LANES), F32),
        ],
        compiler_params=pltpu.CompilerParams(vmem_limit_bytes=38 * 2**20),
        cost_estimate=pl.CostEstimate(flops=10**10, transcendentals=0, bytes_accessed=2 * 10**7),
        name="products",
    )(place, cross, edge, near, *gradient_matrices(), smooth_matrix())


def in_hbm(m):
    return pltpu.with_memory_space_constraint(jnp.asarray(m), pltpu.HBM)


def smooth_matrix():
    bh, bl = halves(z_smooth_matrix())
    return in_hbm(np.concatenate([bh, bh, bl], axis=1))


GROUP = 8


STEP = 2


def smooth_y_kernel(in_ref, m_ref, out_ref):
    lane = lax.broadcasted_iota(jnp.int32, (64, LANES), 1)
    zero = jnp.zeros((64, LANES), F32)

    for c in range(STEP):
        rows = pl.ds(pl.multiple_of(64 * (2 * pl.program_id(0) + c), 64), 64)
        for start in range(0, NB, 2 * GROUP):
            stack = []
            for j in range(start, start + 2 * GROUP, 2):
                before = in_ref[j - 1, rows, :] if j > 0 else zero
                after = in_ref[j + 2, rows, :] if j + 2 < NB else zero
                rims = jnp.where(lane < 64, after, before)
                pair = [in_ref[j, rows, :], in_ref[j + 1, rows, :], rims]
                xh, xl = split(jnp.concatenate(pair, axis=1))
                stack.append(jnp.concatenate([xh, xl, xh], axis=1))
            o = dot(jnp.concatenate(stack, axis=0), m_ref[...])
            for k in range(GROUP):
                j = start + 2 * k
                for x in range(16):
                    first = 64 * k + 4 * x
                    out_ref[c, x, :, 128 * j : 128 * j + 256] = o[first : first + 4, :]


def smooth_y(received):
    mh, ml = halves(y_smooth_matrix())
    m = in_hbm(np.concatenate([mh, mh, ml], axis=0))
    return pl.pallas_call(
        smooth_y_kernel,
        grid=(6 // STEP,),
        out_shape=jax.ShapeDtypeStruct((6, 16, 4, NB * LANES), F32),
        in_specs=[VMEM, VMEM],
        out_specs=pl.BlockSpec((STEP, 16, 4, NB * LANES), lambda i: (i, 0, 0, 0)),
        compiler_params=pltpu.CompilerParams(vmem_limit_bytes=24 * 2**20),
        cost_estimate=pl.CostEstimate(flops=6 * 10**9, transcendentals=0, bytes_accessed=10**7),
        name="smooth_y",
    )(received, m)


def on_device(volume, occupancy):
    message = pack(volume, occupancy)
    columns = lax.all_to_all(message, "dev", 0, 0, tiled=True)
    partner = lax.ppermute(columns, "gx", [(0, 1), (1, 0), (2, 3), (3, 2)])
    cross = lax.ppermute(columns, "gx", [(1, 2), (2, 1)])
    place = lax.axis_index("gx").reshape(1)
    edge, near = near_gradients(place, columns, partner)
    blocks = products(place, cross, edge, near)
    received = lax.all_to_all(blocks, "dev", 0, 0, tiled=True)
    return smooth_y(received)


def solution(mesh):
    return jax.shard_map(
        on_device,
        mesh=mesh,
        in_specs=(P("gx", "dev", None), P("gx", "dev")),
        out_specs=P(None, "gx", "dev", None),
        check_vma=False,
    )
```

```python
import math

import jax
import jax.numpy as jnp
import ml_dtypes
import numpy as np
from jax import lax
from jax.experimental import pallas as pl
from jax.experimental.pallas import tpu as pltpu
from jax.sharding import PartitionSpec as P

RAD_D = 3
RAD_S = 12
SIGMA_DERIV = 1.0
SIGMA_SMOOTH = 4.0

NB = 32
LANES = 128
HALO_SLOT = 16
MSG_ROWS = 72
F32 = jnp.float32
BF16 = jnp.bfloat16


def kernel_taps(radius, width_sigma, derivative):
    offsets = [float(t) for t in range(-radius, radius + 1)]
    weights = [math.exp(-0.5 * (t / width_sigma) ** 2) for t in offsets]
    if derivative:
        total = sum((t * t * w for t, w in zip(offsets, weights)))
        return [t * w / total for t, w in zip(offsets, weights)]
    total = sum(weights)
    return [w / total for w in weights]


G1 = kernel_taps(RAD_D, SIGMA_DERIV, False)
D1 = kernel_taps(RAD_D, SIGMA_DERIV, True)
G4 = kernel_taps(RAD_S, SIGMA_SMOOTH, False)


def halves(matrix):
    high = matrix.astype(ml_dtypes.bfloat16)
    low = (matrix - high.astype(np.float64)).astype(ml_dtypes.bfloat16)
    return high, low


def band(taps, n):
    radius = len(taps) // 2
    m = np.zeros((n, n))
    for i in range(n):
        for t in range(-radius, radius + 1):
            if 0 <= i + t < n:
                m[i, i + t] = taps[t + radius]
    return m


def y_gradient_matrix():
    m = np.zeros((2 * LANES, 2 * LANES))
    for part, taps in enumerate((G1, D1)):
        for y in range(LANES):
            for t in range(-RAD_D, RAD_D + 1):
                s = y + t
                w = taps[t + RAD_D]
                col = part * LANES + y
                if 0 <= s < LANES:
                    m[s, col] = w
                else:
                    k = s + RAD_D if s < 0 else RAD_D + s - LANES
                    for seg in range(8):
                        m[LANES + seg * HALO_SLOT + k, col] = w
    return m


def pair_order():
    return [(xp, 4 * d + z) for d in range(NB) for xp in range(2) for z in range(4)]


def z_gradient_matrix():
    return np.concatenate([band(G1, 128), band(D1, 128)], axis=0)


def z_smooth_matrix():
    smooth = band(G4, 128)
    m = np.zeros((256, 256))
    for row, (xp, z) in enumerate(pair_order()):
        m[row, xp * 128 : xp * 128 + 128] = smooth[z]
    return m


def y_smooth_matrix():
    m = np.zeros((384, 256))
    for y in range(256):
        for t in range(-RAD_S, RAD_S + 1):
            s = y + t
            if s < 0:
                s = 256 + 128 + s
            elif s >= 256:
                s = 256 + s - 256
            m[s, y] = G4[t + RAD_S]
    return m


def split(x):
    high = x.astype(BF16)
    return high, (x - high.astype(F32)).astype(BF16)


def dot(a, b):
    return jnp.dot(a, b, preferred_element_type=F32)


def pack_kernel(occ_ref, vol_ref, out_ref):
    lane = lax.broadcasted_iota(jnp.int32, (8, LANES), 1)
    for p in range(8):
        present = occ_ref[0, p // 4].astype(F32)
        rows = jnp.concatenate([vol_ref[2 * p], vol_ref[2 * p + 1]], axis=0) * present
        blocks = [rows[:, j * LANES : (j + 1) * LANES] for j in range(NB)]
        zero = jnp.zeros((8, LANES), F32)
        for j in range(NB):
            out_ref[j, 8 * p : 8 * p + 8, :] = blocks[j]
            before = blocks[j - 1] if j > 0 else zero
            after = blocks[j + 1] if j < NB - 1 else zero
            rim = jnp.where(lane >= LANES - 3, before, jnp.where(lane < 3, after, 0.0))
            rim = pltpu.roll(rim, 3, 1, stride=HALO_SLOT, stride_axis=0)
            out_ref[j, 64 + p, :] = jnp.sum(rim, axis=0)


def pack(volume, occupancy):
    return pl.pallas_call(
        pack_kernel,
        out_shape=pltpu.VMEM((NB, MSG_ROWS, LANES), F32),
        in_specs=[
            pl.BlockSpec(memory_space=pltpu.SMEM),
            pl.BlockSpec(memory_space=pltpu.VMEM),
        ],
        out_specs=pl.BlockSpec(memory_space=pltpu.VMEM),
        name="pack",
    )(occupancy.T, volume)


NROW = 48
PROWS = 40


def smooth_products(chunk, grads, b_ref, out_ref, sums):
    def along_x(step):
        k = step // 4
        c = chunk[0] + k
        first = (c > 2).astype(jnp.int32) + (c > 4).astype(jnp.int32)
        second = c - 2 * (c > 2).astype(jnp.int32) - (c > 4).astype(jnp.int32)
        for q in range(4):
            rows = pl.ds(pl.multiple_of(32 * (step % 4) + 8 * q, 8), 8)
            col = [grads[first, r, rows, :] * grads[second, r, rows, :] for r in range(PROWS)]
            for x in range(16):
                s = G4[12] * col[x + 12]
                for t in range(1, RAD_S + 1):
                    s = s + G4[12 + t] * (col[x + 12 + t] + col[x + 12 - t])
                sums[k % 2, x, rows, :] = s

    def along_depth(step):
        k, x = step // 4, 4 * (step % 4)
        a = sums[k % 2, pl.ds(x, 2)].reshape(256, LANES)
        b = sums[k % 2, pl.ds(x + 2, 2)].reshape(256, LANES)
        sh, sl = split(jnp.concatenate([a, b], axis=1))
        o = dot(b_ref[...], jnp.concatenate([sh, sl, sh], axis=0))
        first = pl.multiple_of(16 * step, 16)
        out_ref[:, pl.ds(first, 8), :] = o[:, :LANES].reshape(NB, 8, LANES)
        out_ref[:, pl.ds(first + 8, 8), :] = o[:, LANES:].reshape(NB, 8, LANES)

    def end(step, carry):
        along_depth(step)
        return carry

    def begin(step, carry):
        along_x(step)
        return carry

    for k in range(len(chunk)):
        lax.fori_loop(4 * k, 4 * k + 4, begin, 0)
        lax.fori_loop(4 * k, 4 * k + 4, end, 0, unroll=4)


NEAR = 25
FAR = PROWS - NEAR
EDGE = 6


def line_fields(src, base, g_ref, w_ref, fields):
    row = lax.broadcasted_iota(jnp.int32, (8, LANES), 0)
    lane = lax.broadcasted_iota(jnp.int32, (8, LANES), 1)
    mine = (row == lane // HALO_SLOT)[None]

    def pair(p, carry):
        first = pl.multiple_of(8 * p, 8)
        main = src[:, pl.ds(first, 8), :]
        rim = src[:, pl.ds(64 + p, 1), :]
        rim = jnp.where(mine, jnp.broadcast_to(rim, (NB, 8, LANES)), 0.0)
        rows = [main[:, :4].reshape(128, LANES), main[:, 4:].reshape(128, LANES)]
        rims = [rim[:, :4].reshape(128, LANES), rim[:, 4:].reshape(128, LANES)]
        both = jnp.concatenate(
            [jnp.concatenate(rows, axis=0), jnp.concatenate(rims, axis=0)], axis=1
        )
        xh, xl = split(both)
        y = dot(jnp.concatenate([xh, xl, xh], axis=1), g_ref[...])
        yh, yl = split(y)

        def lanes(m, k):
            k = k * LANES
            return jnp.concatenate([m[:128, k : k + LANES], m[128:, k : k + LANES]], axis=1)

        sh, sl = lanes(yh, 0), lanes(yl, 0)
        dh, dl = lanes(yh, 1), lanes(yl, 1)
        both = dot(w_ref[...], jnp.concatenate([sh, sl, sh], axis=0))
        other = dot(w_ref[:128, :], jnp.concatenate([dh, dl, dh], axis=0))
        e = base + 2 * p
        for k in range(2):
            cols = slice(k * LANES, (k + 1) * LANES)
            fields[0, e + k] = both[:128, cols]
            fields[1, e + k] = other[:, cols]
            fields[2, e + k] = both[128:, cols]
        return carry

    lax.fori_loop(0, 8, pair, 0, unroll=8)


def gradient_rows(place, fields, start, count, out, out_start, unroll):
    def one(i, carry):
        r = start + i
        keep = jnp.where((r < 12) & (place == 0), 0.0, 1.0)
        keep = jnp.where((r >= 28) & (place == 3), 0.0, keep)
        for zt in range(16):
            rows = pl.ds(8 * zt, 8)

            def tap(f, t):
                return fields[f, r + (4 + t), rows, :]

            def sym(f):
                s = G1[3] * tap(f, 0)
                for t in (1, 2, 3):
                    s = s + G1[3 + t] * (tap(f, t) + tap(f, -t))
                return s * keep

            gx = D1[4] * (tap(0, 1) - tap(0, -1))
            for t in (2, 3):
                gx = gx + D1[3 + t] * (tap(0, t) - tap(0, -t))
            out[0, out_start + i, rows, :] = gx * keep
            out[1, out_start + i, rows, :] = sym(1)
            out[2, out_start + i, rows, :] = sym(2)
        return carry

    lax.fori_loop(0, count, one, 0, unroll=unroll)


def near_kernel(place_ref, own_ref, partner_ref, g_ref, w_ref, edge_ref, near_ref, fields):
    place = place_ref[0]
    odd = place % 2
    line_fields(own_ref, 16, g_ref, w_ref, fields)
    line_fields(partner_ref, 32 - 32 * odd, g_ref, w_ref, fields)
    for f in range(3):
        for k in range(EDGE):
            edge_ref[f, k] = fields[f, 16 + 10 * odd + k]
    gradient_rows(place, fields, FAR - FAR * odd, NEAR, near_ref, 0, 5)


def far_kernel(
    place_ref, cross_ref, edge_ref, near_ref, g_ref, w_ref, b_ref, out_ref, fields, grads, sums
):
    place = place_ref[0]
    odd = place % 2
    inner = (place == 1) | (place == 2)

    @pl.when(inner)
    def _():
        line_fields(cross_ref, 32 * odd, g_ref, w_ref, fields)

    @pl.when(jnp.logical_not(inner))
    def _():
        zero = jnp.zeros((128, LANES), F32)
        for f in range(3):
            for k in range(16):
                fields[f, 32 * odd + k] = zero

    for f in range(3):
        for k in range(EDGE):
            fields[f, 16 + 10 * odd + k] = edge_ref[f, k]
    far = NEAR * odd
    gradient_rows(place, fields, far, FAR, grads, far, 3)

    def copy(i, carry):
        for f in range(3):
            grads[f, FAR - FAR * odd + i] = near_ref[f, i]
        return carry

    lax.fori_loop(0, NEAR, copy, 0)
    smooth_products(range(6), grads, b_ref, out_ref, sums)


VMEM = pl.BlockSpec(memory_space=pltpu.VMEM)
SMEM = pl.BlockSpec(memory_space=pltpu.SMEM)
FIELDS = pltpu.VMEM((3, NROW, 128, LANES), F32)


def gradient_matrices():
    gh, gl = halves(y_gradient_matrix())
    wh, wl = halves(z_gradient_matrix())
    g = np.concatenate([gh, gh, gl], axis=0)
    w = np.concatenate([wh, wh, wl], axis=1)
    return in_hbm(g), in_hbm(w)


def near_gradients(place, own, partner):
    return pl.pallas_call(
        near_kernel,
        out_shape=(
            pltpu.VMEM((3, EDGE, 128, LANES), F32),
            pltpu.VMEM((3, NEAR, 128, LANES), F32),
        ),
        in_specs=[SMEM] + [VMEM] * 4,
        out_specs=(VMEM, VMEM),
        scratch_shapes=[FIELDS],
        compiler_params=pltpu.CompilerParams(vmem_limit_bytes=30 * 2**20),
        cost_estimate=pl.CostEstimate(flops=10**10, transcendentals=0, bytes_accessed=2 * 10**7),
        name="near",
    )(place, own, partner, *gradient_matrices())


def products(place, cross, edge, near):
    return pl.pallas_call(
        far_kernel,
        out_shape=pltpu.VMEM((NB, 384, LANES), F32),
        in_specs=[SMEM] + [VMEM] * 6,
        out_specs=VMEM,
        scratch_shapes=[
            FIELDS,
            pltpu.VMEM((3, PROWS, 128, LANES), F32),
            pltpu.VMEM((2, 16, 128, LANES), F32),
        ],
        compiler_params=pltpu.CompilerParams(vmem_limit_bytes=38 * 2**20),
        cost_estimate=pl.CostEstimate(flops=10**10, transcendentals=0, bytes_accessed=2 * 10**7),
        name="products",
    )(place, cross, edge, near, *gradient_matrices(), smooth_matrix())


def in_hbm(m):
    return pltpu.with_memory_space_constraint(jnp.asarray(m), pltpu.HBM)


def smooth_matrix():
    bh, bl = halves(z_smooth_matrix())
    return in_hbm(np.concatenate([bh, bh, bl], axis=1))


GROUP = 8


STEP = 2


def smooth_y_kernel(in_ref, m_ref, out_ref):
    lane = lax.broadcasted_iota(jnp.int32, (64, LANES), 1)
    zero = jnp.zeros((64, LANES), F32)

    for c in range(STEP):
        rows = pl.ds(pl.multiple_of(64 * (2 * pl.program_id(0) + c), 64), 64)
        for start in range(0, NB, 2 * GROUP):
            stack = []
            for j in range(start, start + 2 * GROUP, 2):
                before = in_ref[j - 1, rows, :] if j > 0 else zero
                after = in_ref[j + 2, rows, :] if j + 2 < NB else zero
                rims = jnp.where(lane < 64, after, before)
                pair = [in_ref[j, rows, :], in_ref[j + 1, rows, :], rims]
                xh, xl = split(jnp.concatenate(pair, axis=1))
                stack.append(jnp.concatenate([xh, xl, xh], axis=1))
            o = dot(jnp.concatenate(stack, axis=0), m_ref[...])
            for k in range(GROUP):
                j = start + 2 * k
                for x in range(16):
                    first = 64 * k + 4 * x
                    out_ref[c, x, :, 128 * j : 128 * j + 256] = o[first : first + 4, :]


def smooth_y(received):
    mh, ml = halves(y_smooth_matrix())
    m = in_hbm(np.concatenate([mh, mh, ml], axis=0))
    return pl.pallas_call(
        smooth_y_kernel,
        grid=(6 // STEP,),
        out_shape=jax.ShapeDtypeStruct((6, 16, 4, NB * LANES), F32),
        in_specs=[VMEM, VMEM],
        out_specs=pl.BlockSpec((STEP, 16, 4, NB * LANES), lambda i: (i, 0, 0, 0)),
        compiler_params=pltpu.CompilerParams(vmem_limit_bytes=24 * 2**20),
        cost_estimate=pl.CostEstimate(flops=6 * 10**9, transcendentals=0, bytes_accessed=10**7),
        name="smooth_y",
    )(received, m)


def on_device(volume, occupancy):
    message = pack(volume, occupancy)
    columns = lax.all_to_all(message, "dev", 0, 0, tiled=True)
    partner = lax.ppermute(columns, "gx", [(0, 1), (1, 0), (2, 3), (3, 2)])
    cross = lax.ppermute(columns, "gx", [(1, 2), (2, 1)])
    place = lax.axis_index("gx").reshape(1)
    edge, near = near_gradients(place, columns, partner)
    blocks = products(place, cross, edge, near)
    received = lax.all_to_all(blocks, "dev", 0, 0, tiled=True)
    return smooth_y(received)


def solution(mesh):
    return jax.shard_map(
        on_device,
        mesh=mesh,
        in_specs=(P("gx", "dev", None), P("gx", "dev")),
        out_specs=P(None, "gx", "dev", None),
        check_vma=False,
    )
```

```python
import math

import jax
import jax.numpy as jnp
import ml_dtypes
import numpy as np
from jax import lax
from jax.experimental import pallas as pl
from jax.experimental.pallas import tpu as pltpu
from jax.sharding import PartitionSpec as P

RAD_D = 3
RAD_S = 12
SIGMA_DERIV = 1.0
SIGMA_SMOOTH = 4.0

NB = 32
LANES = 128
HALO_SLOT = 16
MSG_ROWS = 72
F32 = jnp.float32
BF16 = jnp.bfloat16


def kernel_taps(radius, width_sigma, derivative):
    offsets = [float(t) for t in range(-radius, radius + 1)]
    weights = [math.exp(-0.5 * (t / width_sigma) ** 2) for t in offsets]
    if derivative:
        total = sum((t * t * w for t, w in zip(offsets, weights)))
        return [t * w / total for t, w in zip(offsets, weights)]
    total = sum(weights)
    return [w / total for w in weights]


G1 = kernel_taps(RAD_D, SIGMA_DERIV, False)
D1 = kernel_taps(RAD_D, SIGMA_DERIV, True)
G4 = kernel_taps(RAD_S, SIGMA_SMOOTH, False)


def halves(matrix):
    high = matrix.astype(ml_dtypes.bfloat16)
    low = (matrix - high.astype(np.float64)).astype(ml_dtypes.bfloat16)
    return high, low


def band(taps, n):
    radius = len(taps) // 2
    m = np.zeros((n, n))
    for i in range(n):
        for t in range(-radius, radius + 1):
            if 0 <= i + t < n:
                m[i, i + t] = taps[t + radius]
    return m


def y_gradient_matrix():
    m = np.zeros((2 * LANES, 2 * LANES))
    for part, taps in enumerate((G1, D1)):
        for y in range(LANES):
            for t in range(-RAD_D, RAD_D + 1):
                s = y + t
                w = taps[t + RAD_D]
                col = part * LANES + y
                if 0 <= s < LANES:
                    m[s, col] = w
                else:
                    k = s + RAD_D if s < 0 else RAD_D + s - LANES
                    for seg in range(8):
                        m[LANES + seg * HALO_SLOT + k, col] = w
    return m


def pair_order():
    return [(xp, 4 * d + z) for d in range(NB) for xp in range(2) for z in range(4)]


def z_gradient_matrix():
    return np.concatenate([band(G1, 128), band(D1, 128)], axis=0)


def z_smooth_matrix():
    smooth = band(G4, 128)
    m = np.zeros((256, 256))
    for row, (xp, z) in enumerate(pair_order()):
        m[row, xp * 128 : xp * 128 + 128] = smooth[z]
    return m


def y_smooth_matrix():
    m = np.zeros((384, 256))
    for y in range(256):
        for t in range(-RAD_S, RAD_S + 1):
            s = y + t
            if s < 0:
                s = 256 + 128 + s
            elif s >= 256:
                s = 256 + s - 256
            m[s, y] = G4[t + RAD_S]
    return m


def split(x):
    high = x.astype(BF16)
    return high, (x - high.astype(F32)).astype(BF16)


def dot(a, b):
    return jnp.dot(a, b, preferred_element_type=F32)


def pack_kernel(occ_ref, vol_ref, out_ref):
    lane = lax.broadcasted_iota(jnp.int32, (8, LANES), 1)
    for p in range(8):
        present = occ_ref[0, p // 4].astype(F32)
        rows = jnp.concatenate([vol_ref[2 * p], vol_ref[2 * p + 1]], axis=0) * present
        blocks = [rows[:, j * LANES : (j + 1) * LANES] for j in range(NB)]
        zero = jnp.zeros((8, LANES), F32)
        for j in range(NB):
            out_ref[j, 8 * p : 8 * p + 8, :] = blocks[j]
            before = blocks[j - 1] if j > 0 else zero
            after = blocks[j + 1] if j < NB - 1 else zero
            rim = jnp.where(lane >= LANES - 3, before, jnp.where(lane < 3, after, 0.0))
            rim = pltpu.roll(rim, 3, 1, stride=HALO_SLOT, stride_axis=0)
            out_ref[j, 64 + p, :] = jnp.sum(rim, axis=0)


def pack(volume, occupancy):
    return pl.pallas_call(
        pack_kernel,
        out_shape=pltpu.VMEM((NB, MSG_ROWS, LANES), F32),
        in_specs=[
            pl.BlockSpec(memory_space=pltpu.SMEM),
            pl.BlockSpec(memory_space=pltpu.VMEM),
        ],
        out_specs=pl.BlockSpec(memory_space=pltpu.VMEM),
        name="pack",
    )(occupancy.T, volume)


NROW = 48
PROWS = 40


def smooth_products(chunk, grads, b_ref, out_ref, sums):
    def along_x(step):
        k = step // 4
        c = chunk[0] + k
        first = (c > 2).astype(jnp.int32) + (c > 4).astype(jnp.int32)
        second = c - 2 * (c > 2).astype(jnp.int32) - (c > 4).astype(jnp.int32)
        for q in range(4):
            rows = pl.ds(pl.multiple_of(32 * (step % 4) + 8 * q, 8), 8)
            col = [grads[first, r, rows, :] * grads[second, r, rows, :] for r in range(PROWS)]
            for x in range(16):
                s = G4[12] * col[x + 12]
                for t in range(1, RAD_S + 1):
                    s = s + G4[12 + t] * (col[x + 12 + t] + col[x + 12 - t])
                sums[k % 2, x, rows, :] = s

    def along_depth(step):
        k, x = step // 4, 4 * (step % 4)
        a = sums[k % 2, pl.ds(x, 2)].reshape(256, LANES)
        b = sums[k % 2, pl.ds(x + 2, 2)].reshape(256, LANES)
        sh, sl = split(jnp.concatenate([a, b], axis=1))
        o = dot(b_ref[...], jnp.concatenate([sh, sl, sh], axis=0))
        first = pl.multiple_of(16 * step, 16)
        out_ref[:, pl.ds(first, 8), :] = o[:, :LANES].reshape(NB, 8, LANES)
        out_ref[:, pl.ds(first + 8, 8), :] = o[:, LANES:].reshape(NB, 8, LANES)

    def end(step, carry):
        along_depth(step)
        return carry

    def begin(step, carry):
        along_x(step)
        return carry

    for k in range(len(chunk)):
        lax.fori_loop(4 * k, 4 * k + 4, begin, 0)
        lax.fori_loop(4 * k, 4 * k + 4, end, 0, unroll=4)


NEAR = 25
FAR = PROWS - NEAR
EDGE = 6


def line_fields(src, base, g_ref, w_ref, fields):
    row = lax.broadcasted_iota(jnp.int32, (8, LANES), 0)
    lane = lax.broadcasted_iota(jnp.int32, (8, LANES), 1)
    mine = (row == lane // HALO_SLOT)[None]

    def pair(p, carry):
        first = pl.multiple_of(8 * p, 8)
        main = src[:, pl.ds(first, 8), :]
        rim = src[:, pl.ds(64 + p, 1), :]
        rim = jnp.where(mine, jnp.broadcast_to(rim, (NB, 8, LANES)), 0.0)
        rows = [main[:, :4].reshape(128, LANES), main[:, 4:].reshape(128, LANES)]
        rims = [rim[:, :4].reshape(128, LANES), rim[:, 4:].reshape(128, LANES)]
        both = jnp.concatenate(
            [jnp.concatenate(rows, axis=0), jnp.concatenate(rims, axis=0)], axis=1
        )
        xh, xl = split(both)
        y = dot(jnp.concatenate([xh, xl, xh], axis=1), g_ref[...])
        yh, yl = split(y)

        def lanes(m, k):
            k = k * LANES
            return jnp.concatenate([m[:128, k : k + LANES], m[128:, k : k + LANES]], axis=1)

        sh, sl = lanes(yh, 0), lanes(yl, 0)
        dh, dl = lanes(yh, 1), lanes(yl, 1)
        both = dot(w_ref[...], jnp.concatenate([sh, sl, sh], axis=0))
        other = dot(w_ref[:128, :], jnp.concatenate([dh, dl, dh], axis=0))
        e = base + 2 * p
        for k in range(2):
            cols = slice(k * LANES, (k + 1) * LANES)
            fields[0, e + k] = both[:128, cols]
            fields[1, e + k] = other[:, cols]
            fields[2, e + k] = both[128:, cols]
        return carry

    lax.fori_loop(0, 8, pair, 0, unroll=8)


def gradient_rows(place, fields, start, count, out, out_start, unroll):
    def one(i, carry):
        r = start + i
        keep = jnp.where((r < 12) & (place == 0), 0.0, 1.0)
        keep = jnp.where((r >= 28) & (place == 3), 0.0, keep)
        for zt in range(16):
            rows = pl.ds(8 * zt, 8)

            def tap(f, t):
                return fields[f, r + (4 + t), rows, :]

            def sym(f):
                s = G1[3] * tap(f, 0)
                for t in (1, 2, 3):
                    s = s + G1[3 + t] * (tap(f, t) + tap(f, -t))
                return s * keep

            gx = D1[4] * (tap(0, 1) - tap(0, -1))
            for t in (2, 3):
                gx = gx + D1[3 + t] * (tap(0, t) - tap(0, -t))
            out[0, out_start + i, rows, :] = gx * keep
            out[1, out_start + i, rows, :] = sym(1)
            out[2, out_start + i, rows, :] = sym(2)
        return carry

    lax.fori_loop(0, count, one, 0, unroll=unroll)


def near_kernel(place_ref, own_ref, partner_ref, g_ref, w_ref, edge_ref, near_ref, fields):
    place = place_ref[0]
    odd = place % 2
    line_fields(own_ref, 16, g_ref, w_ref, fields)
    line_fields(partner_ref, 32 - 32 * odd, g_ref, w_ref, fields)
    for f in range(3):
        for k in range(EDGE):
            edge_ref[f, k] = fields[f, 16 + 10 * odd + k]
    gradient_rows(place, fields, FAR - FAR * odd, NEAR, near_ref, 0, 5)


def far_kernel(
    place_ref, cross_ref, edge_ref, near_ref, g_ref, w_ref, b_ref, out_ref, fields, grads, sums
):
    place = place_ref[0]
    odd = place % 2
    inner = (place == 1) | (place == 2)
    for f in range(3):
        for k in range(EDGE):
            fields[f, 16 + 10 * odd + k] = edge_ref[f, k]
    far = NEAR * odd

    @pl.when(inner)
    def _():
        line_fields(cross_ref, 32 * odd, g_ref, w_ref, fields)
        gradient_rows(place, fields, far, FAR, grads, far, 3)

    @pl.when(jnp.logical_not(inner))
    def _():
        zero = jnp.zeros((128, LANES), F32)
        for f in range(3):
            for k in range(3):
                fields[f, 13 + 19 * odd + k] = zero
            for k in range(12):
                grads[f, 28 * odd + k] = zero
        start = 12 + 13 * odd
        gradient_rows(place, fields, start, 3, grads, start, 3)

    def copy(i, carry):
        for f in range(3):
            grads[f, FAR - FAR * odd + i] = near_ref[f, i]
        return carry

    lax.fori_loop(0, NEAR, copy, 0)
    smooth_products(range(6), grads, b_ref, out_ref, sums)


VMEM = pl.BlockSpec(memory_space=pltpu.VMEM)
SMEM = pl.BlockSpec(memory_space=pltpu.SMEM)
FIELDS = pltpu.VMEM((3, NROW, 128, LANES), F32)


def gradient_matrices():
    gh, gl = halves(y_gradient_matrix())
    wh, wl = halves(z_gradient_matrix())
    g = np.concatenate([gh, gh, gl], axis=0)
    w = np.concatenate([wh, wh, wl], axis=1)
    return in_hbm(g), in_hbm(w)


def near_gradients(place, own, partner):
    return pl.pallas_call(
        near_kernel,
        out_shape=(
            pltpu.VMEM((3, EDGE, 128, LANES), F32),
            pltpu.VMEM((3, NEAR, 128, LANES), F32),
        ),
        in_specs=[SMEM] + [VMEM] * 4,
        out_specs=(VMEM, VMEM),
        scratch_shapes=[FIELDS],
        compiler_params=pltpu.CompilerParams(vmem_limit_bytes=30 * 2**20),
        cost_estimate=pl.CostEstimate(flops=10**10, transcendentals=0, bytes_accessed=2 * 10**7),
        name="near",
    )(place, own, partner, *gradient_matrices())


def products(place, cross, edge, near):
    return pl.pallas_call(
        far_kernel,
        out_shape=pltpu.VMEM((NB, 384, LANES), F32),
        in_specs=[SMEM] + [VMEM] * 6,
        out_specs=VMEM,
        scratch_shapes=[
            FIELDS,
            pltpu.VMEM((3, PROWS, 128, LANES), F32),
            pltpu.VMEM((2, 16, 128, LANES), F32),
        ],
        compiler_params=pltpu.CompilerParams(vmem_limit_bytes=38 * 2**20),
        cost_estimate=pl.CostEstimate(flops=10**10, transcendentals=0, bytes_accessed=2 * 10**7),
        name="products",
    )(place, cross, edge, near, *gradient_matrices(), smooth_matrix())


def in_hbm(m):
    return pltpu.with_memory_space_constraint(jnp.asarray(m), pltpu.HBM)


def smooth_matrix():
    bh, bl = halves(z_smooth_matrix())
    return in_hbm(np.concatenate([bh, bh, bl], axis=1))


GROUP = 8


STEP = 2


def smooth_y_kernel(in_ref, m_ref, out_ref):
    lane = lax.broadcasted_iota(jnp.int32, (64, LANES), 1)
    zero = jnp.zeros((64, LANES), F32)

    for c in range(STEP):
        rows = pl.ds(pl.multiple_of(64 * (2 * pl.program_id(0) + c), 64), 64)
        for start in range(0, NB, 2 * GROUP):
            stack = []
            for j in range(start, start + 2 * GROUP, 2):
                before = in_ref[j - 1, rows, :] if j > 0 else zero
                after = in_ref[j + 2, rows, :] if j + 2 < NB else zero
                rims = jnp.where(lane < 64, after, before)
                pair = [in_ref[j, rows, :], in_ref[j + 1, rows, :], rims]
                xh, xl = split(jnp.concatenate(pair, axis=1))
                stack.append(jnp.concatenate([xh, xl, xh], axis=1))
            o = dot(jnp.concatenate(stack, axis=0), m_ref[...])
            for k in range(GROUP):
                j = start + 2 * k
                for x in range(16):
                    first = 64 * k + 4 * x
                    out_ref[c, x, :, 128 * j : 128 * j + 256] = o[first : first + 4, :]


def smooth_y(received):
    mh, ml = halves(y_smooth_matrix())
    m = in_hbm(np.concatenate([mh, mh, ml], axis=0))
    return pl.pallas_call(
        smooth_y_kernel,
        grid=(6 // STEP,),
        out_shape=jax.ShapeDtypeStruct((6, 16, 4, NB * LANES), F32),
        in_specs=[VMEM, VMEM],
        out_specs=pl.BlockSpec((STEP, 16, 4, NB * LANES), lambda i: (i, 0, 0, 0)),
        compiler_params=pltpu.CompilerParams(vmem_limit_bytes=24 * 2**20),
        cost_estimate=pl.CostEstimate(flops=6 * 10**9, transcendentals=0, bytes_accessed=10**7),
        name="smooth_y",
    )(received, m)


def on_device(volume, occupancy):
    message = pack(volume, occupancy)
    columns = lax.all_to_all(message, "dev", 0, 0, tiled=True)
    partner = lax.ppermute(columns, "gx", [(0, 1), (1, 0), (2, 3), (3, 2)])
    cross = lax.ppermute(columns, "gx", [(1, 2), (2, 1)])
    place = lax.axis_index("gx").reshape(1)
    edge, near = near_gradients(place, columns, partner)
    blocks = products(place, cross, edge, near)
    received = lax.all_to_all(blocks, "dev", 0, 0, tiled=True)
    return smooth_y(received)


def solution(mesh):
    return jax.shard_map(
        on_device,
        mesh=mesh,
        in_specs=(P("gx", "dev", None), P("gx", "dev")),
        out_specs=P(None, "gx", "dev", None),
        check_vma=False,
    )
```
